32 devices in a mesh: groups: 2 (over x), docs: 8 (over z, y), clus: 2 (over core).
Axes of the slice: x: 2, y: 2, z: 4, core: 2. Of those that a mesh axis runs over, the one named last changes fastest.
Arguments:
- embeddings: bfloat16 [8192, 1024], P(('groups', 'docs', 'clus')), parts along dimension 0, may hold values from -6 to 6
- assignment: int32 [8192], P(('groups', 'docs', 'clus')), parts along dimension 0, may hold values from 0 to 255, as said below
Outputs:
- max_similarity: float32 [8192], P(('groups', 'docs', 'clus')), parts along dimension 0
- centre_similarity: float32 [8192], P(('groups', 'docs', 'clus')), parts along dimension 0
The draws below stay inside these ranges and needn't reach their ends.
There are 2 independent parts, one for each index of `groups`. The reference program is written for one: setup_inputs(seed, part) draws one part's arguments, and reference() takes and returns one part's arrays. A program takes and returns all parts, laid end to end along the dimension named above; each array names one. Nothing has to cross between parts.
Inputs may be any that keep to these rules, and one draw needn't show every extreme that they name: `assignment`: cluster c is owned by the device of index c // 16 along docs and clus together. Of the 256 rows of one device, at most 32 are assigned to the clusters of one owner, and some owner gets exactly 32 from every device.
All inputs are finite; a program needn't handle non-finite values.
Results may differ from the reference program's by a relative error of at most 0.0015.
Values may be sent and summed in bfloat16 or wider, within the bound.
A program may use at most 64 MiB of HBM per device.

```python
import jax
import jax.numpy as jnp
from jax import lax

D = 1024
KO = 16
TOK_DEV = 256
TOKENS = 4096
DEVICE_DOC_LIMIT = 32
N_DOCS = 8
N_CLUS = 2


def draw_assignment(key, part):
    key = jax.random.fold_in(key, 7)
    owner_list = N_DOCS * N_CLUS
    sorting_keys = jax.random.split(key, 3)
    reward_extra = jax.random.randint(sorting_keys[0], (owner_list,), 0, 4)
    selected_owner = jax.random.randint(sorting_keys[1], (), 0, owner_list)
    reward_extra = jnp.where(jnp.arange(owner_list) == selected_owner, 64, reward_extra)
    position_owner = jnp.arange(owner_list * DEVICE_DOC_LIMIT, dtype=jnp.int32) // DEVICE_DOC_LIMIT

    def one_block(block_key, home):
        leading_index, second, third = jax.random.split(block_key, 3)
        placement_score = jax.random.randint(leading_index, (owner_list * DEVICE_DOC_LIMIT,), 0, 1 << 20) + reward_extra[position_owner] * (1 << 19)
        picked = jnp.argsort(-placement_score, stable=True)[:TOK_DEV]
        target = jax.random.permutation(second, position_owner[picked])
        is_home = (target == home).astype(jnp.int32)
        lone = (is_home == 1) & (jnp.cumsum(is_home) == 1)
        inner = jax.random.randint(third, (TOK_DEV,), 1, KO)
        inner = jnp.where(lone, 0, inner)
        return target * KO + inner
    blocks = jax.vmap(one_block)(jax.random.split(sorting_keys[2], owner_list), jnp.arange(owner_list, dtype=jnp.int32))
    return blocks.reshape(-1).astype(jnp.int32)


def block_levels(stream_key, shape, cuts, least, largest):
    gain = 1.0
    for axis_at, shards_of in cuts:
        steps = jax.random.uniform(jax.random.fold_in(jax.random.fold_in(stream_key, 6), axis_at), (shards_of,), jnp.float32, least / len(cuts), largest / len(cuts))
        gain = gain * jnp.repeat(jnp.exp(steps), shape[axis_at] // shards_of).reshape((-1,) + (1,) * (len(shape) - 1 - axis_at))
    return gain


def noise(stream_key, dims, scale, reach, shards=(), kind=jnp.bfloat16):
    loudness = block_levels(stream_key, dims, shards, -0.22, 0.18) if shards else 1.0
    values = jax.random.normal(stream_key, dims, jnp.float32) * scale * loudness
    return jnp.minimum(jnp.maximum(values, -reach), reach).astype(kind)


def setup_inputs(seed: int = 0, part: int = 0) -> dict:
    keys = jax.random.split(jax.random.key(seed), 3)
    own_keys = jax.random.split(jax.random.fold_in(keys[2], part), 3)
    return {
        "embeddings": noise(own_keys[0], (TOKENS, D), 1.0, 6.0, ((0, 16),)),
        "assignment": draw_assignment(jax.random.fold_in(jax.random.fold_in(keys[2], part), 71), part),
    }


def reference(embeddings, assignment):
    wide = embeddings.astype(jnp.float32)
    unit = (wide * lax.rsqrt(lax.optimization_barrier(jnp.sum(wide * wide, axis=1, keepdims=True)) + 1e-06)).astype(jnp.bfloat16)
    unit_wide = unit.astype(jnp.float32)
    owner_list = N_DOCS * N_CLUS
    clusters = KO * owner_list
    sums = jax.ops.segment_sum(unit_wide, assignment, num_segments=clusters)
    centre = (sums * lax.rsqrt(lax.optimization_barrier(jnp.sum(sums * sums, axis=1, keepdims=True)) + 1e-06)).astype(jnp.bfloat16)
    centre_similarity = lax.optimization_barrier(jnp.sum(unit_wide * centre[assignment].astype(jnp.float32), axis=1))
    order = jnp.argsort(assignment, stable=True).astype(jnp.int32)
    sorted_ids = assignment[order]
    sorted_owner = sorted_ids // KO
    counts = jax.ops.segment_sum(jnp.ones_like(sorted_owner), sorted_owner, num_segments=owner_list)
    starts = (jnp.cumsum(counts) - counts).astype(jnp.int32)
    window = owner_list * DEVICE_DOC_LIMIT
    padded_rows = jnp.concatenate([unit_wide[order], jnp.zeros((window, D), jnp.float32)], axis=0)
    padded_ids = jnp.concatenate([sorted_ids, jnp.full((window,), -1, jnp.int32)], axis=0)
    positions = jnp.arange(window, dtype=jnp.int32)

    def per_owner(start):
        block = lax.dynamic_slice(padded_rows, (start, jnp.int32(0)), (window, D))
        labels = lax.dynamic_slice(padded_ids, (start,), (window,))
        scores = jnp.dot(block, block.T, precision=lax.Precision.HIGHEST, preferred_element_type=jnp.float32)
        keep = (labels[:, None] == labels[None, :]) & (positions[:, None] != positions[None, :])
        return lax.optimization_barrier(jnp.max(jnp.where(keep, scores, -1.0), axis=1))
    bests = lax.map(per_owner, starts)
    offset = jnp.arange(TOKENS, dtype=jnp.int32) - starts[sorted_owner]
    best_sorted = bests[sorted_owner, offset]
    max_similarity = jnp.zeros((TOKENS,), jnp.float32).at[order].set(best_sorted)
    return (max_similarity, centre_similarity)
```

```python
import functools

import jax
import jax.numpy as jnp
from jax import lax
from jax.experimental import pallas as pl
from jax.experimental.pallas import tpu as pltpu
from jax.sharding import PartitionSpec as P

KO = 16
LANES = 128
MESH = pl.DeviceIdType.MESH


def iota(shape, axis):
    return lax.broadcasted_iota(jnp.int32, shape, axis)


def kernel(
    n,
    cap,
    emb_ref,
    asg_ref,
    best_ref,
    cent_ref,
    out_buf,
    in_buf,
    lab_out,
    lab_in,
    res,
    back,
    row_send,
    row_recv,
    lab_send,
    lab_recv,
    res_send,
    res_recv,
):
    rows, width = emb_ref.shape
    slots = n * cap
    per = LANES // cap
    half = n // 2
    inner_n = lax.axis_size("clus")
    me = lax.axis_index("docs") * inner_n + lax.axis_index("clus")
    my_half = me // half
    far_half = 1 - my_half

    def at(index):
        return {"docs": index // inner_n, "clus": index % inner_n}

    far = [far_half * half + (me + k) % half for k in range(half)]
    near = [my_half * half + (me + k) % half for k in range(1, half)]
    others = far + near

    barrier = pltpu.get_barrier_semaphore()
    for other in others:
        pl.semaphore_signal(barrier, inc=1, device_id=at(other), device_id_type=MESH)

    asg = asg_ref[...]
    owner = lax.div(asg, KO)
    inner = asg - owner * KO
    hit = iota((n, rows), 0) == owner
    marks = hit.astype(jnp.bfloat16)
    earlier = (iota((rows, rows), 0) < iota((rows, rows), 1)).astype(jnp.bfloat16)
    before = jnp.dot(marks, earlier, preferred_element_type=jnp.float32)
    rank = jnp.sum(jnp.where(hit, before, 0.0), axis=0, keepdims=True).astype(jnp.int32)
    target = owner * cap + rank
    lane_hit = iota((LANES, rows), 0) == (me % per) * cap + rank
    lane_marks = lane_hit.astype(jnp.bfloat16)
    named = jnp.where(hit, (inner + 1).astype(jnp.float32), 0.0).astype(jnp.bfloat16)
    lab_out[...] = lax.dot_general(
        named, lane_marks, (((1,), (1,)), ((), ())), preferred_element_type=jnp.float32
    ).reshape(n, 1, LANES)
    lab_in[me] = lab_out[me]

    wide = emb_ref[...].astype(jnp.float32)
    unit = (wide * lax.rsqrt(jnp.sum(wide * wide, axis=1, keepdims=True) + 1e-06)).astype(
        jnp.bfloat16
    )

    def place(which):
        pick = iota((half * cap, rows), 0) + which * (half * cap) == target
        moved = jnp.dot(pick.astype(jnp.bfloat16), unit, preferred_element_type=jnp.float32)
        out_buf[pl.ds(which * half, half)] = moved.astype(jnp.bfloat16).reshape(half, cap, width)

    def row_copy(other, mine):
        return pltpu.make_async_remote_copy(
            src_ref=out_buf.at[other],
            dst_ref=in_buf.at[mine],
            send_sem=row_send.at[other],
            recv_sem=row_recv.at[mine],
            device_id=at(other),
            device_id_type=MESH,
        )

    def lab_copy(other, mine):
        return pltpu.make_async_remote_copy(
            src_ref=lab_out.at[other],
            dst_ref=lab_in.at[mine],
            send_sem=lab_send.at[other],
            recv_sem=lab_recv.at[mine],
            device_id=at(other),
            device_id_type=MESH,
        )

    def res_copy(other, mine):
        return pltpu.make_async_remote_copy(
            src_ref=res.at[other // per],
            dst_ref=back.at[mine],
            send_sem=res_send.at[other],
            recv_sem=res_recv.at[mine],
            device_id=at(other),
            device_id_type=MESH,
        )

    place(far_half)
    pl.semaphore_wait(barrier, len(others))
    for other in others:
        lab_copy(other, me).start()
    for other in far:
        row_copy(other, me).start()
    place(my_half)
    for other in near:
        row_copy(other, me).start()
    in_buf[me] = out_buf[me]

    for other in others:
        lab_copy(other, other).wait_recv()
    tags = jnp.concatenate(
        [jnp.sum(lab_in[q * per : (q + 1) * per], axis=0) for q in range(n // per)], axis=1
    ).astype(jnp.int32)
    tag_hit = iota((KO, slots), 0) + 1 == tags
    hits = tag_hit.astype(jnp.bfloat16)

    for other in near + far:
        row_copy(other, other).wait_recv()

    members = in_buf[...].reshape(slots, width)
    sums = jnp.dot(hits, members, preferred_element_type=jnp.float32)
    centre = (sums * lax.rsqrt(jnp.sum(sums * sums, axis=1, keepdims=True) + 1e-06)).astype(
        jnp.bfloat16
    )
    against = lax.dot_general(
        centre, members, (((1,), (1,)), ((), ())), preferred_element_type=jnp.float32
    )
    cent_row = jnp.sum(jnp.where(tag_hit, against, 0.0), axis=0, keepdims=True)
    same = lax.dot_general(
        hits, hits, (((0,), (0,)), ((), ())), preferred_element_type=jnp.float32
    )
    scores = lax.dot_general(
        members, members, (((1,), (1,)), ((), ())), preferred_element_type=jnp.float32
    )
    keep = (same > 0.5) & (iota((slots, slots), 0) != iota((slots, slots), 1))
    best_row = jnp.max(jnp.where(keep, scores, -1.0), axis=0, keepdims=True)
    for q in range(n // per):
        res[q, 0:1, :] = best_row[:, q * LANES : (q + 1) * LANES]
        res[q, 1:2, :] = cent_row[:, q * LANES : (q + 1) * LANES]

    for other in others:
        res_copy(other, me).start()
    back[me] = res[me // per]
    for other in others:
        res_copy(other, other).wait_recv()

    marks32 = marks.astype(jnp.float32)
    for at_row, out_ref in ((0, best_ref), (1, cent_ref)):
        picked = lax.dot_general(
            back[:, at_row, :],
            marks32,
            (((0,), (0,)), ((), ())),
            precision=lax.Precision.HIGHEST,
            preferred_element_type=jnp.float32,
        )
        out_ref[...] = jnp.sum(jnp.where(lane_hit, picked, 0.0), axis=0, keepdims=True)

    for other in others:
        row_copy(other, me).wait_send()
        lab_copy(other, me).wait_send()
        res_copy(other, me).wait_send()


def fused(embeddings, assignment, n, cap):
    rows, width = embeddings.shape
    per = LANES // cap
    vmem = pl.BlockSpec(memory_space=pltpu.VMEM)
    best, cent = pl.pallas_call(
        functools.partial(kernel, n, cap),
        out_shape=[jax.ShapeDtypeStruct((1, rows), jnp.float32)] * 2,
        in_specs=[vmem, vmem],
        out_specs=[vmem, vmem],
        scratch_shapes=[
            pltpu.VMEM((n, cap, width), jnp.bfloat16),
            pltpu.VMEM((n, cap, width), jnp.bfloat16),
            pltpu.VMEM((n, 1, LANES), jnp.float32),
            pltpu.VMEM((n, 1, LANES), jnp.float32),
            pltpu.VMEM((n // per, 2, LANES), jnp.float32),
            pltpu.VMEM((n, 2, LANES), jnp.float32),
        ]
        + [pltpu.SemaphoreType.DMA((n,))] * 6,
        compiler_params=pltpu.CompilerParams(
            collective_id=0, has_side_effects=True, vmem_limit_bytes=32 * 1024 * 1024
        ),
    )(embeddings, assignment.reshape(1, rows))
    return best.reshape(rows), cent.reshape(rows)


def plain(embeddings, assignment, n, cap):
    rows, width = embeddings.shape
    slots = n * cap
    wide = embeddings.astype(jnp.float32)
    unit = (wide * lax.rsqrt(jnp.sum(wide * wide, axis=1, keepdims=True) + 1e-06)).astype(
        jnp.bfloat16
    )
    owner = assignment // KO
    inner = assignment % KO
    marks = (owner[:, None] == jnp.arange(n, dtype=jnp.int32)[None, :]).astype(jnp.int32)
    before = jnp.cumsum(marks, axis=0) - marks
    target = owner * cap + jnp.sum(before * marks, axis=1)
    outgoing = jnp.zeros((slots, width), jnp.bfloat16).at[target].set(unit)
    labels_out = jnp.full((slots,), -1.0, jnp.bfloat16).at[target].set(inner.astype(jnp.bfloat16))

    def swap(value):
        return lax.all_to_all(
            value, ("docs", "clus"), split_axis=0, concat_axis=0, tiled=True
        )

    members = swap(outgoing.reshape(n, cap, width)).reshape(slots, width)
    tags = swap(labels_out.reshape(n, cap)).reshape(slots).astype(jnp.int32)
    member_hits = tags[:, None] == jnp.arange(KO, dtype=jnp.int32)[None, :]
    sums = lax.dot_general(
        member_hits.astype(jnp.bfloat16),
        members,
        (((0,), (0,)), ((), ())),
        preferred_element_type=jnp.float32,
    )
    centre = (sums * lax.rsqrt(jnp.sum(sums * sums, axis=1, keepdims=True) + 1e-06)).astype(
        jnp.bfloat16
    )
    against = lax.dot_general(
        members, centre, (((1,), (1,)), ((), ())), preferred_element_type=jnp.float32
    )
    centre_part = jnp.sum(jnp.where(member_hits, against, 0.0), axis=1)
    scores = lax.dot_general(
        members, members, (((1,), (1,)), ((), ())), preferred_element_type=jnp.float32
    )
    at = jnp.arange(slots, dtype=jnp.int32)
    keep = (
        (tags[:, None] == tags[None, :])
        & (tags[:, None] >= 0)
        & (at[:, None] != at[None, :])
    )
    best = jnp.max(jnp.where(keep, scores, -1.0), axis=1)
    both = swap(jnp.stack([best.reshape(n, cap), centre_part.reshape(n, cap)], axis=1))
    return (both[:, 0].reshape(slots)[target], both[:, 1].reshape(slots)[target])


def on_device(embeddings, assignment):
    n = lax.axis_size(("docs", "clus"))
    cap = 2 * embeddings.shape[0] // n
    if cap % 16 == 0 and LANES % cap == 0 and n % (LANES // cap) == 0:
        return fused(embeddings, assignment, n, cap)
    return plain(embeddings, assignment, n, cap)


def solution(mesh):
    placed = (P(("groups", "docs", "clus"), None), P(("groups", "docs", "clus")))
    return jax.shard_map(
        on_device,
        mesh=mesh,
        in_specs=placed,
        out_specs=(P(("groups", "docs", "clus")), P(("groups", "docs", "clus"))),
        check_vma=False,
    )
```

```python
import functools

import jax
import jax.numpy as jnp
from jax import lax
from jax.experimental import pallas as pl
from jax.experimental.pallas import tpu as pltpu
from jax.sharding import PartitionSpec as P

KO = 16
LANES = 128
MESH = pl.DeviceIdType.MESH


def iota(shape, axis):
    return lax.broadcasted_iota(jnp.int32, shape, axis)


def kernel(
    n,
    cap,
    emb_hbm,
    asg_hbm,
    both_ref,
    emb_ref,
    asg_ref,
    out_buf,
    in_buf,
    lab_out,
    lab_in,
    res,
    back,
    row_send,
    row_recv,
    lab_send,
    lab_recv,
    res_send,
    res_recv,
    emb_sem,
    asg_sem,
):
    emb_load = pltpu.make_async_copy(emb_hbm, emb_ref, emb_sem)
    asg_load = pltpu.make_async_copy(asg_hbm, asg_ref, asg_sem)
    asg_load.start()
    emb_load.start()
    rows, width = emb_ref.shape
    slots = n * cap
    per = LANES // cap
    half = n // 2
    inner_n = lax.axis_size("clus")
    me = lax.axis_index("docs") * inner_n + lax.axis_index("clus")
    my_half = me // half
    far_half = 1 - my_half

    def at(index):
        return {"docs": index // inner_n, "clus": index % inner_n}

    far = [far_half * half + (me + k) % half for k in range(half)]
    near = [my_half * half + (me + k) % half for k in range(1, half)]
    others = far + near

    barrier = pltpu.get_barrier_semaphore()
    for other in others:
        pl.semaphore_signal(barrier, inc=1, device_id=at(other), device_id_type=MESH)

    asg_load.wait()
    asg = asg_ref[...]
    owner = lax.div(asg, KO)
    inner = asg - owner * KO
    hit = iota((n, rows), 0) == owner
    marks = hit.astype(jnp.bfloat16)
    earlier = (iota((rows, rows), 0) < iota((rows, rows), 1)).astype(jnp.bfloat16)
    before = jnp.dot(marks, earlier, preferred_element_type=jnp.float32)
    rank = jnp.sum(jnp.where(hit, before, 0.0), axis=0, keepdims=True).astype(jnp.int32)
    target = owner * cap + rank
    lane_hit = iota((LANES, rows), 0) == (me % per) * cap + rank
    lane_marks = lane_hit.astype(jnp.bfloat16)
    named = jnp.where(hit, (inner + 1).astype(jnp.float32), 0.0).astype(jnp.bfloat16)
    lab_out[...] = lax.dot_general(
        named, lane_marks, (((1,), (1,)), ((), ())), preferred_element_type=jnp.float32
    ).reshape(n, 1, LANES)
    lab_in[me] = lab_out[me]

    emb_load.wait()
    wide = emb_ref[...].astype(jnp.float32)
    unit = (wide * lax.rsqrt(jnp.sum(wide * wide, axis=1, keepdims=True) + 1e-06)).astype(
        jnp.bfloat16
    )

    def place(which):
        pick = iota((half * cap, rows), 0) + which * (half * cap) == target
        moved = jnp.dot(pick.astype(jnp.bfloat16), unit, preferred_element_type=jnp.float32)
        out_buf[pl.ds(which * half, half)] = moved.astype(jnp.bfloat16).reshape(half, cap, width)

    def whole(src, dst, send_sem, recv_sem):
        return pltpu.make_async_remote_copy(
            src_ref=src.at[pl.ds(0, n - 1)],
            dst_ref=dst.at[pl.ds(0, n - 1)],
            send_sem=send_sem,
            recv_sem=recv_sem,
            device_id=at(others[0]),
            device_id_type=MESH,
        )

    def row_copy(other, mine):
        return pltpu.make_async_remote_copy(
            src_ref=out_buf.at[other],
            dst_ref=in_buf.at[mine],
            send_sem=row_send,
            recv_sem=row_recv,
            device_id=at(other),
            device_id_type=MESH,
        )

    def lab_copy(other, mine):
        return pltpu.make_async_remote_copy(
            src_ref=lab_out.at[other],
            dst_ref=lab_in.at[mine],
            send_sem=lab_send,
            recv_sem=lab_recv,
            device_id=at(other),
            device_id_type=MESH,
        )

    def res_copy(other, mine):
        return pltpu.make_async_remote_copy(
            src_ref=res.at[other // per],
            dst_ref=back.at[mine],
            send_sem=res_send,
            recv_sem=res_recv,
            device_id=at(other),
            device_id_type=MESH,
        )

    place(far_half)
    pl.semaphore_wait(barrier, len(others))
    for other in far:
        row_copy(other, me).start()
    for other in others:
        lab_copy(other, me).start()
    place(my_half)
    for other in near:
        row_copy(other, me).start()
    in_buf[me] = out_buf[me]

    lab_all = whole(lab_out, lab_in, lab_send, lab_recv)
    row_all = whole(out_buf, in_buf, row_send, row_recv)
    res_all = whole(back, back, res_send, res_recv)
    lab_all.wait_recv()
    tags = jnp.concatenate(
        [jnp.sum(lab_in[q * per : (q + 1) * per], axis=0) for q in range(n // per)], axis=1
    ).astype(jnp.int32)
    tag_hit = iota((KO, slots), 0) + 1 == tags
    hits = tag_hit.astype(jnp.bfloat16)

    row_all.wait_recv()

    members = in_buf[...].reshape(slots, width)
    sums = jnp.dot(hits, members, preferred_element_type=jnp.float32)
    centre = (sums * lax.rsqrt(jnp.sum(sums * sums, axis=1, keepdims=True) + 1e-06)).astype(
        jnp.bfloat16
    )
    against = lax.dot_general(
        centre, members, (((1,), (1,)), ((), ())), preferred_element_type=jnp.float32
    )
    cent_row = jnp.sum(jnp.where(tag_hit, against, 0.0), axis=0, keepdims=True)
    same = lax.dot_general(
        hits, hits, (((0,), (0,)), ((), ())), preferred_element_type=jnp.float32
    )
    scores = lax.dot_general(
        members, members, (((1,), (1,)), ((), ())), preferred_element_type=jnp.float32
    )
    keep = (same > 0.5) & (iota((slots, slots), 0) != iota((slots, slots), 1))
    best_row = jnp.max(jnp.where(keep, scores, -1.0), axis=0, keepdims=True)
    for q in range(n // per):
        res[q, 0:1, :] = best_row[:, q * LANES : (q + 1) * LANES]
        res[q, 1:2, :] = cent_row[:, q * LANES : (q + 1) * LANES]

    for other in others:
        res_copy(other, me).start()
    back[me] = res[me // per]
    row_all.wait_send()
    lab_all.wait_send()
    res_all.wait_recv()

    marks32 = marks.astype(jnp.float32)
    for at_row in (0, 1):
        picked = lax.dot_general(
            back[:, at_row, :],
            marks32,
            (((0,), (0,)), ((), ())),
            precision=lax.Precision.HIGHEST,
            preferred_element_type=jnp.float32,
        )
        both_ref[at_row : at_row + 1, :] = jnp.sum(jnp.where(lane_hit, picked, 0.0), axis=0, keepdims=True)

    res_all.wait_send()


def fused(embeddings, assignment, n, cap):
    rows, width = embeddings.shape
    per = LANES // cap
    vmem = pl.BlockSpec(memory_space=pltpu.VMEM)
    hbm = pl.BlockSpec(memory_space=pltpu.HBM)
    both = pl.pallas_call(
        functools.partial(kernel, n, cap),
        out_shape=jax.ShapeDtypeStruct((2, rows), jnp.float32),
        in_specs=[hbm, hbm],
        out_specs=vmem,
        scratch_shapes=[
            pltpu.VMEM((rows, width), jnp.bfloat16),
            pltpu.VMEM((1, rows), jnp.int32),
            pltpu.VMEM((n, cap, width), jnp.bfloat16),
            pltpu.VMEM((n, cap, width), jnp.bfloat16),
            pltpu.VMEM((n, 1, LANES), jnp.float32),
            pltpu.VMEM((n, 1, LANES), jnp.float32),
            pltpu.VMEM((n // per, 2, LANES), jnp.float32),
            pltpu.VMEM((n, 2, LANES), jnp.float32),
        ]
        + [pltpu.SemaphoreType.DMA] * 8,
        compiler_params=pltpu.CompilerParams(
            collective_id=0, has_side_effects=True, vmem_limit_bytes=63 * 1024 * 1024 + 960 * 1024
        ),
    )(embeddings, assignment.reshape(1, rows))
    return both[0], both[1]


def plain(embeddings, assignment, n, cap):
    rows, width = embeddings.shape
    slots = n * cap
    wide = embeddings.astype(jnp.float32)
    unit = (wide * lax.rsqrt(jnp.sum(wide * wide, axis=1, keepdims=True) + 1e-06)).astype(
        jnp.bfloat16
    )
    owner = assignment // KO
    inner = assignment % KO
    marks = (owner[:, None] == jnp.arange(n, dtype=jnp.int32)[None, :]).astype(jnp.int32)
    before = jnp.cumsum(marks, axis=0) - marks
    target = owner * cap + jnp.sum(before * marks, axis=1)
    outgoing = jnp.zeros((slots, width), jnp.bfloat16).at[target].set(unit)
    labels_out = jnp.full((slots,), -1.0, jnp.bfloat16).at[target].set(inner.astype(jnp.bfloat16))

    def swap(value):
        return lax.all_to_all(
            value, ("docs", "clus"), split_axis=0, concat_axis=0, tiled=True
        )

    members = swap(outgoing.reshape(n, cap, width)).reshape(slots, width)
    tags = swap(labels_out.reshape(n, cap)).reshape(slots).astype(jnp.int32)
    member_hits = tags[:, None] == jnp.arange(KO, dtype=jnp.int32)[None, :]
    sums = lax.dot_general(
        member_hits.astype(jnp.bfloat16),
        members,
        (((0,), (0,)), ((), ())),
        preferred_element_type=jnp.float32,
    )
    centre = (sums * lax.rsqrt(jnp.sum(sums * sums, axis=1, keepdims=True) + 1e-06)).astype(
        jnp.bfloat16
    )
    against = lax.dot_general(
        members, centre, (((1,), (1,)), ((), ())), preferred_element_type=jnp.float32
    )
    centre_part = jnp.sum(jnp.where(member_hits, against, 0.0), axis=1)
    scores = lax.dot_general(
        members, members, (((1,), (1,)), ((), ())), preferred_element_type=jnp.float32
    )
    at = jnp.arange(slots, dtype=jnp.int32)
    keep = (
        (tags[:, None] == tags[None, :])
        & (tags[:, None] >= 0)
        & (at[:, None] != at[None, :])
    )
    best = jnp.max(jnp.where(keep, scores, -1.0), axis=1)
    both = swap(jnp.stack([best.reshape(n, cap), centre_part.reshape(n, cap)], axis=1))
    return (both[:, 0].reshape(slots)[target], both[:, 1].reshape(slots)[target])


def on_device(embeddings, assignment):
    n = lax.axis_size(("docs", "clus"))
    cap = 2 * embeddings.shape[0] // n
    if cap % 16 == 0 and LANES % cap == 0 and n % (LANES // cap) == 0:
        return fused(embeddings, assignment, n, cap)
    return plain(embeddings, assignment, n, cap)


def solution(mesh):
    placed = (P(("groups", "docs", "clus"), None), P(("groups", "docs", "clus")))
    return jax.shard_map(
        on_device,
        mesh=mesh,
        in_specs=placed,
        out_specs=(P(("groups", "docs", "clus")), P(("groups", "docs", "clus"))),
        check_vma=False,
    )
```

```python
import functools

import jax
import jax.numpy as jnp
from jax import lax
from jax.experimental import pallas as pl
from jax.experimental.pallas import tpu as pltpu
from jax.sharding import PartitionSpec as P

KO = 16
LANES = 128
MESH = pl.DeviceIdType.MESH


def iota(shape, axis):
    return lax.broadcasted_iota(jnp.int32, shape, axis)


def kernel(
    n,
    cap,
    emb_hbm,
    asg_hbm,
    both_ref,
    emb_ref,
    asg_ref,
    out_buf,
    in_buf,
    lab_out,
    lab_in,
    res,
    back,
    row_send,
    near_recv,
    far_recv,
    lab_send,
    lab_recv,
    res_send,
    res_recv,
    emb_sem,
    asg_sem,
):
    emb_load = pltpu.make_async_copy(emb_hbm, emb_ref, emb_sem)
    asg_load = pltpu.make_async_copy(asg_hbm, asg_ref, asg_sem)
    asg_load.start()
    emb_load.start()
    rows, width = emb_ref.shape
    slots = n * cap
    per = LANES // cap
    half = n // 2
    inner_n = lax.axis_size("clus")
    me = lax.axis_index("docs") * inner_n + lax.axis_index("clus")
    my_half = me // half
    far_half = 1 - my_half

    def at(index):
        return {"docs": index // inner_n, "clus": index % inner_n}

    far = [far_half * half + (me + k) % half for k in range(half)]
    near = [my_half * half + (me + k) % half for k in range(1, half)]
    others = far + near

    barrier = pltpu.get_barrier_semaphore()
    for other in others:
        pl.semaphore_signal(barrier, inc=1, device_id=at(other), device_id_type=MESH)

    asg_load.wait()
    asg = asg_ref[...]
    owner = lax.div(asg, KO)
    inner = asg - owner * KO
    hit = iota((n, rows), 0) == owner
    marks = hit.astype(jnp.bfloat16)
    earlier = (iota((rows, rows), 0) < iota((rows, rows), 1)).astype(jnp.bfloat16)
    before = jnp.dot(marks, earlier, preferred_element_type=jnp.float32)
    rank = jnp.sum(jnp.where(hit, before, 0.0), axis=0, keepdims=True).astype(jnp.int32)
    target = owner * cap + rank
    lane_hit = iota((LANES, rows), 0) == (me % per) * cap + rank
    lane_marks = lane_hit.astype(jnp.bfloat16)
    named = jnp.where(hit, (inner + 1).astype(jnp.float32), 0.0).astype(jnp.bfloat16)
    lab_out[...] = lax.dot_general(
        named, lane_marks, (((1,), (1,)), ((), ())), preferred_element_type=jnp.float32
    ).reshape(n, 1, LANES)
    lab_in[me] = lab_out[me]

    emb_load.wait()
    wide = emb_ref[...].astype(jnp.float32)
    unit = (wide * lax.rsqrt(jnp.sum(wide * wide, axis=1, keepdims=True) + 1e-06)).astype(
        jnp.bfloat16
    )

    def place(which):
        pick = iota((half * cap, rows), 0) + which * (half * cap) == target
        moved = jnp.dot(pick.astype(jnp.bfloat16), unit, preferred_element_type=jnp.float32)
        out_buf[pl.ds(which * half, half)] = moved.astype(jnp.bfloat16).reshape(half, cap, width)

    def whole(src, dst, send_sem, recv_sem, count):
        return pltpu.make_async_remote_copy(
            src_ref=src.at[pl.ds(0, count)],
            dst_ref=dst.at[pl.ds(0, count)],
            send_sem=send_sem,
            recv_sem=recv_sem,
            device_id=at(others[0]),
            device_id_type=MESH,
        )

    def row_copy(other, mine, recv_sem):
        return pltpu.make_async_remote_copy(
            src_ref=out_buf.at[other],
            dst_ref=in_buf.at[mine],
            send_sem=row_send,
            recv_sem=recv_sem,
            device_id=at(other),
            device_id_type=MESH,
        )

    def lab_copy(other, mine):
        return pltpu.make_async_remote_copy(
            src_ref=lab_out.at[other],
            dst_ref=lab_in.at[mine],
            send_sem=lab_send,
            recv_sem=lab_recv,
            device_id=at(other),
            device_id_type=MESH,
        )

    def res_copy(other, mine):
        return pltpu.make_async_remote_copy(
            src_ref=res.at[other // per],
            dst_ref=back.at[mine],
            send_sem=res_send,
            recv_sem=res_recv,
            device_id=at(other),
            device_id_type=MESH,
        )

    place(far_half)
    pl.semaphore_wait(barrier, len(others))
    for other in far[:2]:
        row_copy(other, me, far_recv).start()
    for other in others:
        lab_copy(other, me).start()
    for other in far[2:]:
        row_copy(other, me, far_recv).start()
    place(my_half)
    for other in near:
        row_copy(other, me, near_recv).start()
    in_buf[me] = out_buf[me]

    lab_all = whole(lab_out, lab_in, lab_send, lab_recv, n - 1)
    row_all = whole(out_buf, in_buf, row_send, near_recv, n - 1)
    res_all = whole(back, back, res_send, res_recv, n - 1)
    lab_all.wait_recv()

    def hits_of(which):
        tags = jnp.concatenate(
            [
                jnp.sum(lab_in[pl.ds(which * half + q * per, per)], axis=0)
                for q in range(half // per)
            ],
            axis=1,
        ).astype(jnp.int32)
        hit = iota((KO, half * cap), 0) + 1 == tags
        return hit, hit.astype(jnp.bfloat16)

    def members_of(which):
        return in_buf[pl.ds(which * half, half)].reshape(half * cap, width)

    def across(left, right):
        return lax.dot_general(
            left, right, (((1,), (1,)), ((), ())), preferred_element_type=jnp.float32
        )

    def same(left, right):
        return (
            lax.dot_general(
                left, right, (((0,), (0,)), ((), ())), preferred_element_type=jnp.float32
            )
            > 0.5
        )

    def best_over(keep, scores):
        return jnp.max(jnp.where(keep, scores, -1.0), axis=0, keepdims=True)

    side = half * cap
    apart = iota((side, side), 0) != iota((side, side), 1)
    near_hit, near_hits = hits_of(my_half)
    far_hit, far_hits = hits_of(far_half)
    near_far = same(near_hits, far_hits)
    far_near = same(far_hits, near_hits)
    far_far = same(far_hits, far_hits) & apart

    whole(out_buf, in_buf, row_send, near_recv, half - 1).wait_recv()
    near_rows = members_of(my_half)
    near_sums = jnp.dot(near_hits, near_rows, preferred_element_type=jnp.float32)
    near_best = best_over(same(near_hits, near_hits) & apart, across(near_rows, near_rows))

    whole(out_buf, in_buf, row_send, far_recv, half).wait_recv()
    near_rows = members_of(my_half)
    far_rows = members_of(far_half)
    sums = near_sums + jnp.dot(far_hits, far_rows, preferred_element_type=jnp.float32)
    near_best = jnp.maximum(near_best, best_over(far_near, across(far_rows, near_rows)))
    far_best = jnp.maximum(
        best_over(near_far, across(near_rows, far_rows)),
        best_over(far_far, across(far_rows, far_rows)),
    )
    centre = (sums * lax.rsqrt(jnp.sum(sums * sums, axis=1, keepdims=True) + 1e-06)).astype(
        jnp.bfloat16
    )
    for which, hit_of, rows_of, best_row in (
        (far_half, far_hit, far_rows, far_best),
        (my_half, near_hit, near_rows, near_best),
    ):
        cent_row = jnp.sum(
            jnp.where(hit_of, across(centre, rows_of), 0.0), axis=0, keepdims=True
        )
        for q in range(half // per):
            chunk = which * (half // per) + q
            res[chunk, 0:1, :] = best_row[:, q * LANES : (q + 1) * LANES]
            res[chunk, 1:2, :] = cent_row[:, q * LANES : (q + 1) * LANES]

    for other in others:
        res_copy(other, me).start()
    back[me] = res[me // per]
    row_all.wait_send()
    lab_all.wait_send()
    res_all.wait_recv()

    marks32 = marks.astype(jnp.float32)
    for at_row in (0, 1):
        picked = lax.dot_general(
            back[:, at_row, :],
            marks32,
            (((0,), (0,)), ((), ())),
            precision=lax.Precision.HIGHEST,
            preferred_element_type=jnp.float32,
        )
        both_ref[at_row : at_row + 1, :] = jnp.sum(jnp.where(lane_hit, picked, 0.0), axis=0, keepdims=True)

    res_all.wait_send()


def fused(embeddings, assignment, n, cap):
    rows, width = embeddings.shape
    per = LANES // cap
    vmem = pl.BlockSpec(memory_space=pltpu.VMEM)
    hbm = pl.BlockSpec(memory_space=pltpu.HBM)
    both = pl.pallas_call(
        functools.partial(kernel, n, cap),
        out_shape=jax.ShapeDtypeStruct((2, rows), jnp.float32),
        in_specs=[hbm, hbm],
        out_specs=vmem,
        scratch_shapes=[
            pltpu.VMEM((rows, width), jnp.bfloat16),
            pltpu.VMEM((1, rows), jnp.int32),
            pltpu.VMEM((n, cap, width), jnp.bfloat16),
            pltpu.VMEM((n, cap, width), jnp.bfloat16),
            pltpu.VMEM((n, 1, LANES), jnp.float32),
            pltpu.VMEM((n, 1, LANES), jnp.float32),
            pltpu.VMEM((n // per, 2, LANES), jnp.float32),
            pltpu.VMEM((n, 2, LANES), jnp.float32),
        ]
        + [pltpu.SemaphoreType.DMA] * 9,
        compiler_params=pltpu.CompilerParams(
            collective_id=0, has_side_effects=True, vmem_limit_bytes=63 * 1024 * 1024 + 960 * 1024
        ),
    )(embeddings, assignment.reshape(1, rows))
    return both[0], both[1]


def plain(embeddings, assignment, n, cap):
    rows, width = embeddings.shape
    slots = n * cap
    wide = embeddings.astype(jnp.float32)
    unit = (wide * lax.rsqrt(jnp.sum(wide * wide, axis=1, keepdims=True) + 1e-06)).astype(
        jnp.bfloat16
    )
    owner = assignment // KO
    inner = assignment % KO
    marks = (owner[:, None] == jnp.arange(n, dtype=jnp.int32)[None, :]).astype(jnp.int32)
    before = jnp.cumsum(marks, axis=0) - marks
    target = owner * cap + jnp.sum(before * marks, axis=1)
    outgoing = jnp.zeros((slots, width), jnp.bfloat16).at[target].set(unit)
    labels_out = jnp.full((slots,), -1.0, jnp.bfloat16).at[target].set(inner.astype(jnp.bfloat16))

    def swap(value):
        return lax.all_to_all(
            value, ("docs", "clus"), split_axis=0, concat_axis=0, tiled=True
        )

    members = swap(outgoing.reshape(n, cap, width)).reshape(slots, width)
    tags = swap(labels_out.reshape(n, cap)).reshape(slots).astype(jnp.int32)
    member_hits = tags[:, None] == jnp.arange(KO, dtype=jnp.int32)[None, :]
    sums = lax.dot_general(
        member_hits.astype(jnp.bfloat16),
        members,
        (((0,), (0,)), ((), ())),
        preferred_element_type=jnp.float32,
    )
    centre = (sums * lax.rsqrt(jnp.sum(sums * sums, axis=1, keepdims=True) + 1e-06)).astype(
        jnp.bfloat16
    )
    against = lax.dot_general(
        members, centre, (((1,), (1,)), ((), ())), preferred_element_type=jnp.float32
    )
    centre_part = jnp.sum(jnp.where(member_hits, against, 0.0), axis=1)
    scores = lax.dot_general(
        members, members, (((1,), (1,)), ((), ())), preferred_element_type=jnp.float32
    )
    at = jnp.arange(slots, dtype=jnp.int32)
    keep = (
        (tags[:, None] == tags[None, :])
        & (tags[:, None] >= 0)
        & (at[:, None] != at[None, :])
    )
    best = jnp.max(jnp.where(keep, scores, -1.0), axis=1)
    both = swap(jnp.stack([best.reshape(n, cap), centre_part.reshape(n, cap)], axis=1))
    return (both[:, 0].reshape(slots)[target], both[:, 1].reshape(slots)[target])


def on_device(embeddings, assignment):
    n = lax.axis_size(("docs", "clus"))
    cap = 2 * embeddings.shape[0] // n
    if cap % 16 == 0 and LANES % cap == 0 and n % (2 * (LANES // cap)) == 0:
        return fused(embeddings, assignment, n, cap)
    return plain(embeddings, assignment, n, cap)


def solution(mesh):
    placed = (P(("groups", "docs", "clus"), None), P(("groups", "docs", "clus")))
    return jax.shard_map(
        on_device,
        mesh=mesh,
        in_specs=placed,
        out_specs=(P(("groups", "docs", "clus")), P(("groups", "docs", "clus"))),
        check_vma=False,
    )
```

```python
import functools

import jax
import jax.numpy as jnp
from jax import lax
from jax.experimental import pallas as pl
from jax.experimental.pallas import tpu as pltpu
from jax.sharding import PartitionSpec as P

KO = 16
LANES = 128
MESH = pl.DeviceIdType.MESH


def iota(shape, axis):
    return lax.broadcasted_iota(jnp.int32, shape, axis)


def kernel(
    n,
    cap,
    emb_hbm,
    asg_hbm,
    both_ref,
    emb_ref,
    asg_ref,
    out_buf,
    in_buf,
    lab_out,
    lab_in,
    res,
    back,
    row_send,
    near_recv,
    far_recv,
    lab_send,
    lab_recv,
    res_send,
    res_recv,
    emb_sem,
    asg_sem,
):
    emb_load = pltpu.make_async_copy(emb_hbm, emb_ref, emb_sem)
    asg_load = pltpu.make_async_copy(asg_hbm, asg_ref, asg_sem)
    asg_load.start()
    emb_load.start()
    rows, width = emb_ref.shape
    slots = n * cap
    per = LANES // cap
    half = n // 2
    inner_n = lax.axis_size("clus")
    me = lax.axis_index("docs") * inner_n + lax.axis_index("clus")
    my_half = me // half
    far_half = 1 - my_half

    def at(index):
        return {"docs": index // inner_n, "clus": index % inner_n}

    far = [far_half * half + (me + k) % half for k in range(half)]
    near = [my_half * half + (me + k) % half for k in range(1, half)]
    others = far + near

    barrier = pltpu.get_barrier_semaphore()
    for other in others:
        pl.semaphore_signal(barrier, inc=1, device_id=at(other), device_id_type=MESH)

    asg_load.wait()
    asg = asg_ref[...]
    owner = lax.div(asg, KO)
    inner = asg - owner * KO
    hit = iota((n, rows), 0) == owner
    marks = hit.astype(jnp.bfloat16)
    earlier = (iota((rows, rows), 0) < iota((rows, rows), 1)).astype(jnp.bfloat16)
    before = jnp.dot(marks, earlier, preferred_element_type=jnp.float32)
    rank = jnp.sum(jnp.where(hit, before, 0.0), axis=0, keepdims=True).astype(jnp.int32)
    target = owner * cap + rank
    lane_hit = iota((LANES, rows), 0) == (me % per) * cap + rank
    lane_marks = lane_hit.astype(jnp.bfloat16)
    named = jnp.where(hit, (inner + 1).astype(jnp.float32), 0.0).astype(jnp.bfloat16)
    lab_out[...] = lax.dot_general(
        named, lane_marks, (((1,), (1,)), ((), ())), preferred_element_type=jnp.float32
    ).reshape(n, 1, LANES)
    lab_in[me] = lab_out[me]

    emb_load.wait()
    wide = emb_ref[...].astype(jnp.float32)
    unit = (wide * lax.rsqrt(jnp.sum(wide * wide, axis=1, keepdims=True) + 1e-06)).astype(
        jnp.bfloat16
    )

    def place(which):
        pick = iota((half * cap, rows), 0) + which * (half * cap) == target
        moved = jnp.dot(pick.astype(jnp.bfloat16), unit, preferred_element_type=jnp.float32)
        out_buf[pl.ds(which * half, half)] = moved.astype(jnp.bfloat16).reshape(half, cap, width)

    def whole(src, dst, send_sem, recv_sem, count):
        return pltpu.make_async_remote_copy(
            src_ref=src.at[pl.ds(0, count)],
            dst_ref=dst.at[pl.ds(0, count)],
            send_sem=send_sem,
            recv_sem=recv_sem,
            device_id=at(others[0]),
            device_id_type=MESH,
        )

    def row_copy(other, mine, recv_sem):
        return pltpu.make_async_remote_copy(
            src_ref=out_buf.at[other],
            dst_ref=in_buf.at[mine],
            send_sem=row_send,
            recv_sem=recv_sem,
            device_id=at(other),
            device_id_type=MESH,
        )

    def lab_copy(other, mine):
        return pltpu.make_async_remote_copy(
            src_ref=lab_out.at[other],
            dst_ref=lab_in.at[mine],
            send_sem=lab_send,
            recv_sem=lab_recv,
            device_id=at(other),
            device_id_type=MESH,
        )

    def res_copy(other, mine):
        return pltpu.make_async_remote_copy(
            src_ref=res.at[other // per],
            dst_ref=back.at[mine],
            send_sem=res_send,
            recv_sem=res_recv,
            device_id=at(other),
            device_id_type=MESH,
        )

    place(far_half)
    pl.semaphore_wait(barrier, len(others))
    for other in far[:2]:
        row_copy(other, me, far_recv).start()
    for other in others:
        lab_copy(other, me).start()
    for other in far[2:]:
        row_copy(other, me, far_recv).start()
    place(my_half)
    for other in near:
        row_copy(other, me, near_recv).start()
    in_buf[me] = out_buf[me]

    lab_all = whole(lab_out, lab_in, lab_send, lab_recv, n - 1)
    row_all = whole(out_buf, in_buf, row_send, near_recv, n - 1)
    res_all = whole(back, back, res_send, res_recv, n - 1)
    lab_all.wait_recv()

    def hits_of(which):
        tags = jnp.concatenate(
            [
                jnp.sum(lab_in[pl.ds(which * half + q * per, per)], axis=0)
                for q in range(half // per)
            ],
            axis=1,
        ).astype(jnp.int32)
        hit = iota((KO, half * cap), 0) + 1 == tags
        return hit, hit.astype(jnp.bfloat16)

    def members_of(which):
        return in_buf[pl.ds(which * half, half)].reshape(half * cap, width)

    def across(left, right):
        return lax.dot_general(
            left, right, (((1,), (1,)), ((), ())), preferred_element_type=jnp.float32
        )

    def same(left, right):
        return (
            lax.dot_general(
                left, right, (((0,), (0,)), ((), ())), preferred_element_type=jnp.float32
            )
            > 0.5
        )

    def best_over(keep, scores):
        return jnp.max(jnp.where(keep, scores, -1.0), axis=0, keepdims=True)

    side = half * cap
    apart = iota((side, side), 0) != iota((side, side), 1)
    near_hit, near_hits = hits_of(my_half)
    far_hit, far_hits = hits_of(far_half)
    near_far = same(near_hits, far_hits)
    far_near = same(far_hits, near_hits)
    far_far = same(far_hits, far_hits) & apart

    whole(out_buf, in_buf, row_send, near_recv, half - 1).wait_recv()
    near_rows = members_of(my_half)
    near_sums = jnp.dot(near_hits, near_rows, preferred_element_type=jnp.float32)
    near_best = best_over(same(near_hits, near_hits) & apart, across(near_rows, near_rows))

    whole(out_buf, in_buf, row_send, far_recv, half).wait_recv()
    near_rows = members_of(my_half)
    far_rows = members_of(far_half)
    sums = near_sums + jnp.dot(far_hits, far_rows, preferred_element_type=jnp.float32)
    near_best = jnp.maximum(near_best, best_over(far_near, across(far_rows, near_rows)))
    far_best = jnp.maximum(
        best_over(near_far, across(near_rows, far_rows)),
        best_over(far_far, across(far_rows, far_rows)),
    )
    centre = (sums * lax.rsqrt(jnp.sum(sums * sums, axis=1, keepdims=True) + 1e-06)).astype(
        jnp.bfloat16
    )
    for which, hit_of, rows_of, best_row in (
        (far_half, far_hit, far_rows, far_best),
        (my_half, near_hit, near_rows, near_best),
    ):
        cent_row = jnp.sum(
            jnp.where(hit_of, across(centre, rows_of), 0.0), axis=0, keepdims=True
        )
        for q in range(half // per):
            chunk = which * (half // per) + q
            res[chunk, 0:1, :] = best_row[:, q * LANES : (q + 1) * LANES]
            res[chunk, 1:2, :] = cent_row[:, q * LANES : (q + 1) * LANES]

    for other in others:
        res_copy(other, me).start()
    back[me] = res[me // per]
    row_all.wait_send()
    lab_all.wait_send()
    res_all.wait_recv()

    rest = jnp.concatenate([back[:, 0, :], back[:, 1, :]], axis=1)
    parts = []
    for _ in range(3):
        parts.append(rest.astype(jnp.bfloat16))
        rest = rest - parts[-1].astype(jnp.float32)
    picked = lax.dot_general(
        jnp.concatenate(parts, axis=0),
        jnp.concatenate([marks] * 3, axis=0),
        (((0,), (0,)), ((), ())),
        preferred_element_type=jnp.float32,
    )
    for at_row in (0, 1):
        lanes = picked[at_row * LANES : (at_row + 1) * LANES]
        both_ref[:, at_row * rows : (at_row + 1) * rows] = jnp.sum(
            jnp.where(lane_hit, lanes, 0.0), axis=0, keepdims=True
        )

    res_all.wait_send()


def fused(embeddings, assignment, n, cap):
    rows, width = embeddings.shape
    per = LANES // cap
    vmem = pl.BlockSpec(memory_space=pltpu.VMEM)
    hbm = pl.BlockSpec(memory_space=pltpu.HBM)
    both = pl.pallas_call(
        functools.partial(kernel, n, cap),
        out_shape=jax.ShapeDtypeStruct((1, 2 * rows), jnp.float32),
        in_specs=[hbm, hbm],
        out_specs=vmem,
        scratch_shapes=[
            pltpu.VMEM((rows, width), jnp.bfloat16),
            pltpu.VMEM((1, rows), jnp.int32),
            pltpu.VMEM((n, cap, width), jnp.bfloat16),
            pltpu.VMEM((n, cap, width), jnp.bfloat16),
            pltpu.VMEM((n, 1, LANES), jnp.float32),
            pltpu.VMEM((n, 1, LANES), jnp.float32),
            pltpu.VMEM((n // per, 2, LANES), jnp.float32),
            pltpu.VMEM((n, 2, LANES), jnp.float32),
        ]
        + [pltpu.SemaphoreType.DMA] * 9,
        compiler_params=pltpu.CompilerParams(
            collective_id=0, has_side_effects=True, vmem_limit_bytes=63 * 1024 * 1024 + 960 * 1024
        ),
    )(embeddings, assignment.reshape(1, rows))
    both = both.reshape(2 * rows)
    return both[:rows], both[rows:]


def plain(embeddings, assignment, n, cap):
    rows, width = embeddings.shape
    slots = n * cap
    wide = embeddings.astype(jnp.float32)
    unit = (wide * lax.rsqrt(jnp.sum(wide * wide, axis=1, keepdims=True) + 1e-06)).astype(
        jnp.bfloat16
    )
    owner = assignment // KO
    inner = assignment % KO
    marks = (owner[:, None] == jnp.arange(n, dtype=jnp.int32)[None, :]).astype(jnp.int32)
    before = jnp.cumsum(marks, axis=0) - marks
    target = owner * cap + jnp.sum(before * marks, axis=1)
    outgoing = jnp.zeros((slots, width), jnp.bfloat16).at[target].set(unit)
    labels_out = jnp.full((slots,), -1.0, jnp.bfloat16).at[target].set(inner.astype(jnp.bfloat16))

    def swap(value):
        return lax.all_to_all(
            value, ("docs", "clus"), split_axis=0, concat_axis=0, tiled=True
        )

    members = swap(outgoing.reshape(n, cap, width)).reshape(slots, width)
    tags = swap(labels_out.reshape(n, cap)).reshape(slots).astype(jnp.int32)
    member_hits = tags[:, None] == jnp.arange(KO, dtype=jnp.int32)[None, :]
    sums = lax.dot_general(
        member_hits.astype(jnp.bfloat16),
        members,
        (((0,), (0,)), ((), ())),
        preferred_element_type=jnp.float32,
    )
    centre = (sums * lax.rsqrt(jnp.sum(sums * sums, axis=1, keepdims=True) + 1e-06)).astype(
        jnp.bfloat16
    )
    against = lax.dot_general(
        members, centre, (((1,), (1,)), ((), ())), preferred_element_type=jnp.float32
    )
    centre_part = jnp.sum(jnp.where(member_hits, against, 0.0), axis=1)
    scores = lax.dot_general(
        members, members, (((1,), (1,)), ((), ())), preferred_element_type=jnp.float32
    )
    at = jnp.arange(slots, dtype=jnp.int32)
    keep = (
        (tags[:, None] == tags[None, :])
        & (tags[:, None] >= 0)
        & (at[:, None] != at[None, :])
    )
    best = jnp.max(jnp.where(keep, scores, -1.0), axis=1)
    both = swap(jnp.stack([best.reshape(n, cap), centre_part.reshape(n, cap)], axis=1))
    return (both[:, 0].reshape(slots)[target], both[:, 1].reshape(slots)[target])


def on_device(embeddings, assignment):
    n = lax.axis_size(("docs", "clus"))
    cap = 2 * embeddings.shape[0] // n
    if cap % 16 == 0 and LANES % cap == 0 and n % (2 * (LANES // cap)) == 0:
        return fused(embeddings, assignment, n, cap)
    return plain(embeddings, assignment, n, cap)


def solution(mesh):
    placed = (P(("groups", "docs", "clus"), None), P(("groups", "docs", "clus")))
    return jax.shard_map(
        on_device,
        mesh=mesh,
        in_specs=placed,
        out_specs=(P(("groups", "docs", "clus")), P(("groups", "docs", "clus"))),
        check_vma=False,
    )
```

```python
import functools

import jax
import jax.numpy as jnp
from jax import lax
from jax.experimental import pallas as pl
from jax.experimental.pallas import tpu as pltpu
from jax.sharding import PartitionSpec as P

KO = 16
LANES = 128
MESH = pl.DeviceIdType.MESH


def iota(shape, axis):
    return lax.broadcasted_iota(jnp.int32, shape, axis)


def kernel(
    n,
    cap,
    emb_hbm,
    asg_hbm,
    both_ref,
    emb_ref,
    asg_ref,
    out_buf,
    in_buf,
    lab_out,
    lab_in,
    res,
    back,
    row_send,
    near_recv,
    far_recv,
    lab_send,
    lab_recv,
    res_send,
    res_recv,
    emb_sem,
    asg_sem,
):
    emb_load = pltpu.make_async_copy(emb_hbm, emb_ref, emb_sem)
    asg_load = pltpu.make_async_copy(asg_hbm, asg_ref, asg_sem)
    rows, width = emb_ref.shape
    slots = n * cap
    per = LANES // cap
    half = n // 2
    inner_n = lax.axis_size("clus")
    me = lax.axis_index("docs") * inner_n + lax.axis_index("clus")
    my_half = me // half
    far_half = 1 - my_half

    def at(index):
        return {"docs": index // inner_n, "clus": index % inner_n}

    far = [far_half * half + (me + k) % half for k in range(half)]
    near = [my_half * half + (me + k) % half for k in range(1, half)]
    others = far + near

    barrier = pltpu.get_barrier_semaphore()
    for other in others:
        pl.semaphore_signal(barrier, inc=1, device_id=at(other), device_id_type=MESH)
    asg_load.start()
    emb_load.start()

    asg_load.wait()
    asg = asg_ref[...]
    owner = lax.div(asg, KO)
    inner = asg - owner * KO
    hit = iota((n, rows), 0) == owner
    marks = hit.astype(jnp.bfloat16)
    earlier = (iota((rows, rows), 0) < iota((rows, rows), 1)).astype(jnp.bfloat16)
    before = jnp.dot(marks, earlier, preferred_element_type=jnp.float32)
    rank = jnp.sum(jnp.where(hit, before, 0.0), axis=0, keepdims=True).astype(jnp.int32)
    target = owner * cap + rank
    lane_hit = iota((LANES, rows), 0) == (me % per) * cap + rank
    lane_marks = lane_hit.astype(jnp.bfloat16)
    named = jnp.where(hit, (inner + 1).astype(jnp.float32), 0.0).astype(jnp.bfloat16)
    lab_out[...] = lax.dot_general(
        named, lane_marks, (((1,), (1,)), ((), ())), preferred_element_type=jnp.float32
    ).reshape(n, 1, LANES)
    lab_in[me] = lab_out[me]

    emb_load.wait()
    wide = emb_ref[...].astype(jnp.float32)
    unit = (wide * lax.rsqrt(jnp.sum(wide * wide, axis=1, keepdims=True) + 1e-06)).astype(
        jnp.bfloat16
    )

    def place(which):
        pick = iota((half * cap, rows), 0) + which * (half * cap) == target
        moved = jnp.dot(pick.astype(jnp.bfloat16), unit, preferred_element_type=jnp.float32)
        out_buf[pl.ds(which * half, half)] = moved.astype(jnp.bfloat16).reshape(half, cap, width)

    def whole(src, dst, send_sem, recv_sem, count):
        return pltpu.make_async_remote_copy(
            src_ref=src.at[pl.ds(0, count)],
            dst_ref=dst.at[pl.ds(0, count)],
            send_sem=send_sem,
            recv_sem=recv_sem,
            device_id=at(others[0]),
            device_id_type=MESH,
        )

    def row_copy(other, mine, recv_sem):
        return pltpu.make_async_remote_copy(
            src_ref=out_buf.at[other],
            dst_ref=in_buf.at[mine],
            send_sem=row_send,
            recv_sem=recv_sem,
            device_id=at(other),
            device_id_type=MESH,
        )

    def lab_copy(other, mine):
        return pltpu.make_async_remote_copy(
            src_ref=lab_out.at[other],
            dst_ref=lab_in.at[mine],
            send_sem=lab_send,
            recv_sem=lab_recv,
            device_id=at(other),
            device_id_type=MESH,
        )

    def res_copy(other, mine):
        return pltpu.make_async_remote_copy(
            src_ref=res.at[other // per],
            dst_ref=back.at[mine],
            send_sem=res_send,
            recv_sem=res_recv,
            device_id=at(other),
            device_id_type=MESH,
        )

    place(far_half)
    place(my_half)
    pl.semaphore_wait(barrier, len(others))
    for other in far[:2]:
        row_copy(other, me, far_recv).start()
    for other in others:
        lab_copy(other, me).start()
    for other in far[2:]:
        row_copy(other, me, far_recv).start()
    for other in near:
        row_copy(other, me, near_recv).start()
    in_buf[me] = out_buf[me]

    lab_all = whole(lab_out, lab_in, lab_send, lab_recv, n - 1)
    row_all = whole(out_buf, in_buf, row_send, near_recv, n - 1)
    res_all = whole(back, back, res_send, res_recv, n - 1)
    lab_all.wait_recv()

    def hits_of(which):
        tags = jnp.concatenate(
            [
                jnp.sum(lab_in[pl.ds(which * half + q * per, per)], axis=0)
                for q in range(half // per)
            ],
            axis=1,
        ).astype(jnp.int32)
        hit = iota((KO, half * cap), 0) + 1 == tags
        return hit, hit.astype(jnp.bfloat16)

    def members_of(which):
        return in_buf[pl.ds(which * half, half)].reshape(half * cap, width)

    def across(left, right):
        return lax.dot_general(
            left, right, (((1,), (1,)), ((), ())), preferred_element_type=jnp.float32
        )

    def same(left, right):
        return (
            lax.dot_general(
                left, right, (((0,), (0,)), ((), ())), preferred_element_type=jnp.float32
            )
            > 0.5
        )

    def best_over(keep, scores):
        return jnp.max(jnp.where(keep, scores, -1.0), axis=0, keepdims=True)

    side = half * cap
    apart = iota((side, side), 0) != iota((side, side), 1)
    near_hit, near_hits = hits_of(my_half)
    far_hit, far_hits = hits_of(far_half)
    near_far = same(near_hits, far_hits)
    far_near = same(far_hits, near_hits)
    far_far = same(far_hits, far_hits) & apart

    whole(out_buf, in_buf, row_send, near_recv, half - 1).wait_recv()
    near_rows = members_of(my_half)
    near_sums = jnp.dot(near_hits, near_rows, preferred_element_type=jnp.float32)
    near_best = best_over(same(near_hits, near_hits) & apart, across(near_rows, near_rows))

    whole(out_buf, in_buf, row_send, far_recv, half).wait_recv()
    near_rows = members_of(my_half)
    far_rows = members_of(far_half)
    sums = near_sums + jnp.dot(far_hits, far_rows, preferred_element_type=jnp.float32)
    far_best = jnp.maximum(
        best_over(near_far, across(near_rows, far_rows)),
        best_over(far_far, across(far_rows, far_rows)),
    )
    centre = (sums * lax.rsqrt(jnp.sum(sums * sums, axis=1, keepdims=True) + 1e-06)).astype(
        jnp.bfloat16
    )
    for which, hit_of, rows_of, best_row in (
        (far_half, far_hit, far_rows, far_best),
        (my_half, near_hit, near_rows, near_best),
    ):
        if which is my_half:
            best_row = jnp.maximum(
                best_row, best_over(far_near, across(far_rows, near_rows))
            )
        cent_row = jnp.sum(
            jnp.where(hit_of, across(centre, rows_of), 0.0), axis=0, keepdims=True
        )
        for q in range(half // per):
            chunk = which * (half // per) + q
            res[chunk, 0:1, :] = best_row[:, q * LANES : (q + 1) * LANES]
            res[chunk, 1:2, :] = cent_row[:, q * LANES : (q + 1) * LANES]
        if which is far_half:
            for other in far:
                res_copy(other, me).start()

    for other in near:
        res_copy(other, me).start()
    back[me] = res[me // per]
    row_all.wait_send()
    lab_all.wait_send()
    res_all.wait_recv()

    rest = jnp.concatenate([back[:, 0, :], back[:, 1, :]], axis=1)
    parts = []
    for _ in range(3):
        parts.append(rest.astype(jnp.bfloat16))
        rest = rest - parts[-1].astype(jnp.float32)
    picked = lax.dot_general(
        jnp.concatenate(parts, axis=0),
        jnp.concatenate([marks] * 3, axis=0),
        (((0,), (0,)), ((), ())),
        preferred_element_type=jnp.float32,
    )
    for at_row in (0, 1):
        lanes = picked[at_row * LANES : (at_row + 1) * LANES]
        both_ref[:, at_row * rows : (at_row + 1) * rows] = jnp.sum(
            jnp.where(lane_hit, lanes, 0.0), axis=0, keepdims=True
        )

    res_all.wait_send()


def fused(embeddings, assignment, n, cap):
    rows, width = embeddings.shape
    per = LANES // cap
    vmem = pl.BlockSpec(memory_space=pltpu.VMEM)
    hbm = pl.BlockSpec(memory_space=pltpu.HBM)
    both = pl.pallas_call(
        functools.partial(kernel, n, cap),
        out_shape=jax.ShapeDtypeStruct((1, 2 * rows), jnp.float32),
        in_specs=[hbm, hbm],
        out_specs=vmem,
        scratch_shapes=[
            pltpu.VMEM((rows, width), jnp.bfloat16),
            pltpu.VMEM((1, rows), jnp.int32),
            pltpu.VMEM((n, cap, width), jnp.bfloat16),
            pltpu.VMEM((n, cap, width), jnp.bfloat16),
            pltpu.VMEM((n, 1, LANES), jnp.float32),
            pltpu.VMEM((n, 1, LANES), jnp.float32),
            pltpu.VMEM((n // per, 2, LANES), jnp.float32),
            pltpu.VMEM((n, 2, LANES), jnp.float32),
        ]
        + [pltpu.SemaphoreType.DMA] * 9,
        compiler_params=pltpu.CompilerParams(
            collective_id=0, has_side_effects=True, vmem_limit_bytes=63 * 1024 * 1024 + 960 * 1024
        ),
    )(embeddings, assignment.reshape(1, rows))
    both = both.reshape(2 * rows)
    return both[:rows], both[rows:]


def plain(embeddings, assignment, n, cap):
    rows, width = embeddings.shape
    slots = n * cap
    wide = embeddings.astype(jnp.float32)
    unit = (wide * lax.rsqrt(jnp.sum(wide * wide, axis=1, keepdims=True) + 1e-06)).astype(
        jnp.bfloat16
    )
    owner = assignment // KO
    inner = assignment % KO
    marks = (owner[:, None] == jnp.arange(n, dtype=jnp.int32)[None, :]).astype(jnp.int32)
    before = jnp.cumsum(marks, axis=0) - marks
    target = owner * cap + jnp.sum(before * marks, axis=1)
    outgoing = jnp.zeros((slots, width), jnp.bfloat16).at[target].set(unit)
    labels_out = jnp.full((slots,), -1.0, jnp.bfloat16).at[target].set(inner.astype(jnp.bfloat16))

    def swap(value):
        return lax.all_to_all(
            value, ("docs", "clus"), split_axis=0, concat_axis=0, tiled=True
        )

    members = swap(outgoing.reshape(n, cap, width)).reshape(slots, width)
    tags = swap(labels_out.reshape(n, cap)).reshape(slots).astype(jnp.int32)
    member_hits = tags[:, None] == jnp.arange(KO, dtype=jnp.int32)[None, :]
    sums = lax.dot_general(
        member_hits.astype(jnp.bfloat16),
        members,
        (((0,), (0,)), ((), ())),
        preferred_element_type=jnp.float32,
    )
    centre = (sums * lax.rsqrt(jnp.sum(sums * sums, axis=1, keepdims=True) + 1e-06)).astype(
        jnp.bfloat16
    )
    against = lax.dot_general(
        members, centre, (((1,), (1,)), ((), ())), preferred_element_type=jnp.float32
    )
    centre_part = jnp.sum(jnp.where(member_hits, against, 0.0), axis=1)
    scores = lax.dot_general(
        members, members, (((1,), (1,)), ((), ())), preferred_element_type=jnp.float32
    )
    at = jnp.arange(slots, dtype=jnp.int32)
    keep = (
        (tags[:, None] == tags[None, :])
        & (tags[:, None] >= 0)
        & (at[:, None] != at[None, :])
    )
    best = jnp.max(jnp.where(keep, scores, -1.0), axis=1)
    both = swap(jnp.stack([best.reshape(n, cap), centre_part.reshape(n, cap)], axis=1))
    return (both[:, 0].reshape(slots)[target], both[:, 1].reshape(slots)[target])


def on_device(embeddings, assignment):
    n = lax.axis_size(("docs", "clus"))
    cap = 2 * embeddings.shape[0] // n
    if cap % 16 == 0 and LANES % cap == 0 and n % (2 * (LANES // cap)) == 0:
        return fused(embeddings, assignment, n, cap)
    return plain(embeddings, assignment, n, cap)


def solution(mesh):
    placed = (P(("groups", "docs", "clus"), None), P(("groups", "docs", "clus")))
    return jax.shard_map(
        on_device,
        mesh=mesh,
        in_specs=placed,
        out_specs=(P(("groups", "docs", "clus")), P(("groups", "docs", "clus"))),
        check_vma=False,
    )
```
